32 devices in a mesh: view: 4 (over z), tm: 8 (over y, x, core).
Axes of the slice: x: 2, y: 2, z: 4, core: 2. Of those that a mesh axis runs over, the one named last changes fastest.
Arguments:
- frames: bfloat16 [4, 32, 160, 640], P('view', 'tm'), may hold values from -6 to 6
- ln_gain: float32 [640], replicated, may hold values from 0.1 to 1.9
- w_query: bfloat16 [640, 640], replicated, as said below
- w_key: bfloat16 [640, 640], replicated, as said below
- w_value: bfloat16 [640, 640], replicated, may hold values from -0.25 to 0.25
- w_out: bfloat16 [640, 640], replicated, may hold values from -1 to 1
- conv_gain: float32 [640], replicated, may hold values from 0.1 to 1.9
- conv_weight: bfloat16 [1920, 640], P('tm'), may hold values from -0.25 to 0.25
Outputs:
- block_out: bfloat16 [4, 32, 160, 640], P('view', 'tm')
The draws below stay inside these ranges and needn't reach their ends.
Inputs may be any that keep to these rules, and one draw needn't show every extreme that they name: `w_query`: a projection matrix. `w_key`: a projection matrix.
All inputs are finite; a program needn't handle non-finite values.
Results may differ from the reference program's by a relative error of at most 0.006.
The reference program's roundings to bfloat16 on the way (of `normed`, `weights`, `attended`, `hidden` and `activated`) count: a program that leaves them out, or rounds other values in their place, can miss the bound.
Values may be sent and summed in bfloat16 or wider, within the bound.
A program may use at most 64 MiB of HBM per device.

```python
import jax
import jax.numpy as jnp
from jax import lax

HEADS = 10
HEAD_DIM = 64
C = 640
TOK = 160
VIEWS = 4
FRAMES = 32


def shared_projections(key):
    base = jax.random.normal(jax.random.fold_in(key, 11), (C, C), jnp.float32)
    noise = jax.random.normal(jax.random.fold_in(key, 12), (C, C), jnp.float32)
    scale = C ** (-0.5)
    first = 2.0 * scale * base
    second = 2.0 * scale * noise
    return (first, second)


def draw_w_query(key, part):
    first, second = shared_projections(key)
    return first.astype(jnp.bfloat16)


def draw_w_key(key, part):
    first, second = shared_projections(key)
    return second.astype(jnp.bfloat16)


def shard_levels(key, extent, split, least, high):
    level = 1.0
    for axis_at, shards_of in split:
        draws = jax.random.uniform(jax.random.fold_in(jax.random.fold_in(key, 6), axis_at), (shards_of,), jnp.float32, least / len(split), high / len(split))
        level = level * jnp.repeat(jnp.exp(draws), extent[axis_at] // shards_of).reshape((-1,) + (1,) * (len(extent) - 1 - axis_at))
    return level


def bell_draw(key, shape, deviation, most, cuts=(), dtype=jnp.bfloat16):
    loudness = shard_levels(key, shape, cuts, -0.22, 0.18) if cuts else 1.0
    array = jax.random.normal(key, shape, jnp.float32) * deviation * loudness
    return jnp.minimum(jnp.maximum(array, -most), most).astype(dtype)


def setup_inputs(seed: int = 0) -> dict:
    seeds = jax.random.split(jax.random.key(seed), 9)
    return {
        "frames": bell_draw(seeds[0], (VIEWS, FRAMES, TOK, C), 1.0, 6.0, ((0, 4), (1, 8))),
        "ln_gain": jnp.clip(1.0 + 0.18 * jax.random.normal(seeds[1], (C,), jnp.float32), 0.1, 1.9),
        "w_query": draw_w_query(jax.random.fold_in(seeds[8], 71), 0),
        "w_key": draw_w_key(jax.random.fold_in(seeds[8], 71), 0),
        "w_value": bell_draw(seeds[4], (C, C), C ** -0.5, 0.25),
        "w_out": bell_draw(seeds[5], (C, C), (C // 16) ** -0.5, 1.0),
        "conv_gain": jnp.clip(1.0 + 0.18 * jax.random.normal(seeds[6], (C,), jnp.float32), 0.1, 1.9),
        "conv_weight": bell_draw(seeds[7], (3 * C, C), C ** -0.5, 0.25, ((0, 8),)),
    }


def layer_norm(values, gain):
    mean = lax.optimization_barrier(jnp.mean(values, axis=-1, keepdims=True))
    centred = values - mean
    variance = lax.optimization_barrier(jnp.mean(centred * centred, axis=-1, keepdims=True))
    return centred * lax.rsqrt(variance + 1e-05) * gain

def attend(query, keyset, valueset):
    rows = query.shape[0]
    heads_q = query.reshape(rows, HEADS, HEAD_DIM).transpose(1, 0, 2)
    heads_k = keyset.reshape(keyset.shape[0], HEADS, HEAD_DIM).transpose(1, 0, 2)
    heads_v = valueset.reshape(valueset.shape[0], HEADS, HEAD_DIM).transpose(1, 0, 2)

    def one_head(trio):
        head_q, head_k, head_v = trio
        scores = jnp.dot(head_q, head_k.T, preferred_element_type=jnp.float32) * HEAD_DIM ** (-0.5)
        top = lax.optimization_barrier(jnp.max(scores, axis=-1, keepdims=True))
        expo = jnp.exp(scores - top)
        weights = (expo / lax.optimization_barrier(jnp.sum(expo, axis=-1, keepdims=True))).astype(jnp.bfloat16)
        return jnp.dot(weights, head_v, preferred_element_type=jnp.float32)
    outputs = lax.map(one_head, (heads_q, heads_k, heads_v))
    return outputs.transpose(1, 0, 2).reshape(rows, HEADS * HEAD_DIM).astype(jnp.bfloat16)

def reference(frames, ln_gain, w_query, w_key, w_value, w_out, conv_gain, conv_weight):
    tokens = frames.astype(jnp.float32)
    normed = layer_norm(tokens, ln_gain).astype(jnp.bfloat16)
    flat = normed.reshape(-1, C)
    query = jnp.dot(flat, w_query, preferred_element_type=jnp.float32).astype(jnp.bfloat16).reshape(normed.shape)
    keys = jnp.dot(flat, w_key, preferred_element_type=jnp.float32).astype(jnp.bfloat16).reshape(normed.shape)
    values = jnp.dot(flat, w_value, preferred_element_type=jnp.float32).astype(jnp.bfloat16).reshape(normed.shape)
    prev_keys = jnp.concatenate([keys[:, :1], keys[:, :-1]], axis=1)
    prev_values = jnp.concatenate([values[:, :1], values[:, :-1]], axis=1)
    anchor_keys = keys[0, 0]
    anchor_values = values[0, 0]

    def one_frame(trio):
        frame_q, frame_k, frame_v = trio
        keyset = jnp.concatenate([anchor_keys, frame_k], axis=0)
        valueset = jnp.concatenate([anchor_values, frame_v], axis=0)
        return attend(frame_q, keyset, valueset)
    attended = lax.map(one_frame, (query.reshape(-1, TOK, C), prev_keys.reshape(-1, TOK, C), prev_values.reshape(-1, TOK, C)))
    mixed = jnp.dot(attended.reshape(-1, C), w_out, preferred_element_type=jnp.float32).reshape(tokens.shape)
    hidden = (tokens + mixed).astype(jnp.bfloat16)
    activated = jax.nn.silu(layer_norm(hidden.astype(jnp.float32), conv_gain)).astype(jnp.bfloat16)
    zeros = jnp.zeros_like(activated[:, :1])
    before = jnp.concatenate([zeros, activated[:, :-1]], axis=1)
    after = jnp.concatenate([activated[:, 1:], zeros], axis=1)
    stacked = jnp.concatenate([before, activated, after], axis=-1).reshape(-1, 3 * C)
    conv = jnp.dot(stacked, conv_weight, preferred_element_type=jnp.float32).reshape(tokens.shape)
    return (hidden.astype(jnp.float32) + conv).astype(jnp.bfloat16)
```

```python
import functools

import jax
import jax.numpy as jnp
from jax import lax
from jax.experimental import pallas as pl
from jax.experimental.pallas import tpu as pltpu
from jax.sharding import PartitionSpec as P

HEAD_DIM = 64
PAIR = 2 * HEAD_DIM
MESH = pl.DeviceIdType.MESH
F32, BF16 = jnp.float32, jnp.bfloat16


def layer_norm(values, gain):
    mean = jnp.mean(values, axis=-1, keepdims=True)
    centred = values - mean
    variance = jnp.mean(centred * centred, axis=-1, keepdims=True)
    return centred * lax.rsqrt(variance + 1e-05) * gain


def mm(a, b):
    return jnp.dot(a, b, preferred_element_type=F32)


def remote(src, dst, send, recv, view, tm):
    return pltpu.make_async_remote_copy(
        src_ref=src, dst_ref=dst, send_sem=send, recv_sem=recv, device_id=(view, tm), device_id_type=MESH
    )


def kernel(nv, nt, pieces, gather,
           fr, ln_gain, wq_h, wk_h, wv_h, wo_h, conv_gain, cw,
           out, x, wq, wk, wv, wo, side, normed, q2, kb, vb, ka, va, att, hid, act, wf,
           load, s1, s2, s3, ra, sp, rp, sw1, rw1, sw2, rw2, sh, rh):
    v, j = lax.axis_index("view"), lax.axis_index("tm")
    nf, tok, width = x.shape
    part = tok // pieces
    shard = cw.shape[0]
    groups = nt // 2
    a, b = j // 2, lax.rem(j, 2)
    sibling = a * 2 + 1 - b
    anc, prev = side.at[0], side.at[1]
    root = (v == 0) & (j == 0)
    holder = (j < pieces) & jnp.logical_not(root)
    other = lax.rem(j + 1, nt)

    loads = [
        pltpu.make_async_copy(fr.at[0], x, load.at[0]),
        pltpu.make_async_copy(wq_h, wq, load.at[1]),
        pltpu.make_async_copy(wk_h, wk, load.at[2]),
        pltpu.make_async_copy(wv_h, wv, load.at[3]),
        pltpu.make_async_copy(wo_h, wo, load.at[4]),
    ]
    for c in loads:
        c.start()
    if gather:
        own_rows = pl.ds(pl.multiple_of(j * shard, 16), shard)
        own_w = pltpu.make_async_copy(cw, wf.at[own_rows], load.at[5])
    else:
        own_w = pltpu.make_async_copy(cw, wf, load.at[5])
    own_w.start()

    barrier = pltpu.get_barrier_semaphore()

    @pl.loop(0, nt)
    def _(t):
        @pl.when(t != j)
        def _():
            pl.semaphore_signal(barrier, inc=1, device_id=(v, t), device_id_type=MESH)

    @pl.loop(0, nv)
    def _(t):
        @pl.when(t != v)
        def _():
            pl.semaphore_signal(barrier, inc=1, device_id=(t, j), device_id_type=MESH)

    pl.semaphore_wait(barrier, nt - 1 + nv - 1)

    def rows(p):
        return pl.ds(pl.multiple_of(p * part, part), part)

    def spread(p, src, act_on):
        @pl.when(v == 0)
        def _():
            @pl.loop(1, nv)
            def _(t):
                act_on(remote(src, anc.at[rows(p)], s2.at[t], ra.at[p], t, j))

        @pl.loop(0, nt)
        def _(t):
            @pl.when((t != j) & ((v != 0) | (t != 0)))
            def _():
                act_on(remote(src, anc.at[rows(p)], s3.at[t], ra.at[p], v, t))

    def scatter(act_on):
        @pl.loop(1, pieces)
        def _(p):
            act_on(remote(fr.at[0, 0, rows(p)], anc.at[rows(p)], s1.at[p], ra.at[p], 0, p))

    def begin(c):
        c.start()

    def sent(c):
        c.wait_send()

    def landed(p):
        remote(anc.at[rows(p)], anc.at[rows(p)], s1.at[p], ra.at[p], v, other).wait_recv()

    def forward():
        landed(j)
        spread(j, anc.at[rows(j)], begin)

    own_anchor = pltpu.make_async_copy(fr.at[0, 0], anc, load.at[6])
    own_prev = pltpu.make_async_copy(fr.at[0, 0], prev, load.at[7])
    to_next = remote(fr.at[0, nf - 1], prev, sp, rp, v, other)

    @pl.when(root)
    def _():
        scatter(begin)
        spread(0, fr.at[0, 0, rows(0)], begin)
        own_anchor.start()

    @pl.when(j < nt - 1)
    def _():
        to_next.start()

    @pl.when(j == 0)
    def _():
        own_prev.start()

    gain = ln_gain[...]
    loads[0].wait()

    @pl.loop(0, nf)
    def _(f):
        normed[pl.ds(pl.multiple_of(f * tok, tok), tok), :] = layer_norm(x[f].astype(F32), gain).astype(BF16)

    @pl.when(holder & (v == 0))
    def _():
        forward()

    lane = lax.broadcasted_iota(jnp.int32, (1, width), 1)
    low = jnp.where(lax.rem(lane, PAIR) < HEAD_DIM, 1.0, 0.0).astype(F32)
    loads[1].wait()
    query = mm(normed[...], wq[...]) * HEAD_DIM ** (-0.5)
    for f in range(nf):
        block = query[f * tok:(f + 1) * tok]
        q2[f, 0:tok, :] = (block * low).astype(BF16)
        q2[f, tok:2 * tok, :] = (block * (1.0 - low)).astype(BF16)
    loads[2].wait()
    loads[3].wait()
    if nf > 1:
        inner = (nf - 1) * tok
        kb[tok:nf * tok, :] = mm(normed[0:inner, :], wk[...]).astype(BF16)
        vb[tok:nf * tok, :] = mm(normed[0:inner, :], wv[...]).astype(BF16)

    @pl.when(holder & (v != 0))
    def _():
        forward()

    def across(act_on):
        @pl.loop(0, groups)
        def _(t):
            @pl.when(t != a)
            def _():
                act_on(remote(cw, wf.at[own_rows], sw1.at[t], rw1.at[a], v, t * 2 + b))

    def shard_rows(t, side_of):
        return pl.ds(pl.multiple_of((t * 2 + side_of) * shard, 16), shard)

    def to_sibling(t):
        return remote(wf.at[shard_rows(t, b)], wf.at[shard_rows(t, b)], sw2.at[t], rw2.at[t], v, sibling)

    if gather:
        across(begin)
        own_w.wait()
        to_sibling(a).start()

    @pl.when(j == 0)
    def _():
        own_prev.wait()

    @pl.when(j > 0)
    def _():
        to_next.wait_recv()

    @pl.when(root)
    def _():
        own_anchor.wait()

    @pl.when(jnp.logical_not(root))
    def _():
        @pl.loop(0, pieces)
        def _(p):
            @pl.when(p != j)
            def _():
                landed(p)

    sides = layer_norm(side[...].astype(F32).reshape(2 * tok, width), gain).astype(BF16)
    keys = mm(sides, wk[...]).astype(BF16)
    values = mm(sides, wv[...]).astype(BF16)
    ka[...] = keys[0:tok]
    va[...] = values[0:tok]
    kb[0:tok, :] = keys[tok:2 * tok]
    vb[0:tok, :] = values[tok:2 * tok]

    loads[4].wait()
    c_gain = conv_gain[...]
    first_half = lax.broadcasted_iota(jnp.int32, (1, PAIR), 1) < HEAD_DIM
    to_right = remote(act.at[pl.ds(nf * tok, tok)], act.at[pl.ds(0, tok)], sh.at[0], rh.at[0], v, other)
    left = lax.rem(j + nt - 1, nt)
    to_left = remote(act.at[pl.ds(tok, tok)], act.at[pl.ds((nf + 1) * tok, tok)], sh.at[1], rh.at[1], v, left)

    @pl.loop(0, nf)
    def _(i):
        f = lax.rem(i + nf - 1, nf)
        if gather:
            @pl.when(i == nf - 1)
            def _():
                @pl.loop(0, groups)
                def _(t):
                    @pl.when(t != a)
                    def _():
                        remote(cw, wf.at[shard_rows(t, b)], sw1.at[t], rw1.at[t], v, other).wait_recv()
                        to_sibling(t).start()

        frame = pl.ds(pl.multiple_of(f * tok, tok), tok)
        for h in range(width // PAIR):
            cols = slice(h * PAIR, (h + 1) * PAIR)
            keyset = jnp.concatenate([ka[:, cols], kb[frame, cols]], axis=0)
            valueset = jnp.concatenate([va[:, cols], vb[frame, cols]], axis=0)
            scores = lax.dot_general(
                q2[f, :, cols], keyset, (((1,), (1,)), ((), ())), preferred_element_type=F32
            )
            expo = jnp.exp(scores - jnp.max(scores, axis=-1, keepdims=True))
            total = jnp.sum(expo, axis=-1, keepdims=True)
            mixed = mm(expo.astype(BF16), valueset) / total
            att[:, cols] = jnp.where(first_half, mixed[0:tok], mixed[tok:2 * tok]).astype(BF16)
        hidden = (x[f].astype(F32) + mm(att[...], wo[...])).astype(BF16)
        hid[frame, :] = hidden
        normal = layer_norm(hidden.astype(F32), c_gain)
        act[pl.ds(pl.multiple_of((f + 1) * tok, tok), tok), :] = (normal * jax.nn.sigmoid(normal)).astype(BF16)

        @pl.when((i == 0) & (j < nt - 1))
        def _():
            to_right.start()

        @pl.when((f == 0) & (j > 0))
        def _():
            to_left.start()

    @pl.when(j == 0)
    def _():
        act[0:tok, :] = jnp.zeros((tok, width), BF16)

    @pl.when(j > 0)
    def _():
        to_right.wait_recv()

    @pl.when(j == nt - 1)
    def _():
        act[(nf + 1) * tok:(nf + 2) * tok, :] = jnp.zeros((tok, width), BF16)

    @pl.when(j < nt - 1)
    def _():
        to_left.wait_recv()

    if gather:
        @pl.loop(0, groups)
        def _(t):
            remote(cw, wf.at[shard_rows(t, 1 - b)], sw2.at[t], rw2.at[t], v, other).wait_recv()
    else:
        own_w.wait()

    total = hid[...].astype(F32)
    for tap in range(3):
        total += mm(act[tap * tok:(tap + nf) * tok, :], wf[tap * width:(tap + 1) * width, :])
    out[...] = total.astype(BF16).reshape(out.shape)

    @pl.when(root)
    def _():
        scatter(sent)
        spread(0, fr.at[0, 0, rows(0)], sent)

    @pl.when(holder)
    def _():
        spread(j, anc.at[rows(j)], sent)

    @pl.when(j < nt - 1)
    def _():
        to_next.wait_send()
        to_right.wait_send()

    @pl.when(j > 0)
    def _():
        to_left.wait_send()

    if gather:
        across(sent)

        @pl.loop(0, groups)
        def _(t):
            to_sibling(t).wait_send()


def solution(mesh):
    nv, nt = mesh.shape["view"], mesh.shape["tm"]

    def per_device(frames, ln_gain, w_query, w_key, w_value, w_out, conv_gain, conv_weight):
        _, nf, tok, width = frames.shape
        shard = conv_weight.shape[0]
        gather = nt % 2 == 0 and shard % 16 == 0
        if not gather:
            conv_weight = lax.all_gather(conv_weight, "tm", axis=0, tiled=True)
        pieces = max(n for n in range(1, nt + 1) if tok % (16 * n) == 0)
        anywhere = pl.BlockSpec(memory_space=pl.ANY)
        vmem = pl.BlockSpec(memory_space=pltpu.VMEM)
        square = pltpu.VMEM((width, width), BF16)
        dma = pltpu.SemaphoreType.DMA
        return pl.pallas_call(
            functools.partial(kernel, nv, nt, pieces, gather),
            out_shape=jax.ShapeDtypeStruct(frames.shape, BF16),
            in_specs=[anywhere, vmem, anywhere, anywhere, anywhere, anywhere, vmem, anywhere],
            out_specs=vmem,
            scratch_shapes=[
                pltpu.VMEM((nf, tok, width), BF16),
                square, square, square, square,
                pltpu.VMEM((2, tok, width), BF16),
                pltpu.VMEM((nf * tok, width), BF16),
                pltpu.VMEM((nf, 2 * tok, width), BF16),
                pltpu.VMEM((nf * tok, width), BF16),
                pltpu.VMEM((nf * tok, width), BF16),
                pltpu.VMEM((tok, width), BF16),
                pltpu.VMEM((tok, width), BF16),
                pltpu.VMEM((tok, width), BF16),
                pltpu.VMEM((nf * tok, width), BF16),
                pltpu.VMEM(((nf + 2) * tok, width), BF16),
                pltpu.VMEM((3 * width, width), BF16),
                dma((8,)), dma((pieces,)), dma((nv,)), dma((nt,)), dma((pieces,)),
                dma, dma,
                dma((nt,)), dma((nt,)), dma((nt,)), dma((nt,)), dma((2,)), dma((2,)),
            ],
            compiler_params=pltpu.CompilerParams(
                collective_id=0, has_side_effects=True, vmem_limit_bytes=60 * 1024 * 1024
            ),
        )(frames, ln_gain[None], w_query, w_key, w_value, w_out, conv_gain[None], conv_weight)

    placed = (P("view", "tm", None, None), P(), P(), P(), P(), P(), P(), P("tm", None))
    return jax.shard_map(
        per_device, mesh=mesh, in_specs=placed, out_specs=P("view", "tm", None, None), check_vma=False
    )
```

```python
import functools

import jax
import jax.numpy as jnp
from jax import lax
from jax.experimental import pallas as pl
from jax.experimental.pallas import tpu as pltpu
from jax.sharding import PartitionSpec as P

HEAD_DIM = 64
PAIR = 2 * HEAD_DIM
MESH = pl.DeviceIdType.MESH
F32, BF16 = jnp.float32, jnp.bfloat16


def layer_norm(values, gain):
    mean = jnp.mean(values, axis=-1, keepdims=True)
    centred = values - mean
    variance = jnp.mean(centred * centred, axis=-1, keepdims=True)
    return centred * lax.rsqrt(variance + 1e-05) * gain


def mm(a, b):
    return jnp.dot(a, b, preferred_element_type=F32)


def remote(src, dst, send, recv, view, tm):
    return pltpu.make_async_remote_copy(
        src_ref=src, dst_ref=dst, send_sem=send, recv_sem=recv, device_id=(view, tm), device_id_type=MESH
    )


def kernel(nv, nt, pieces, gather,
           fr, ln_gain, wq_h, wk_h, wv_h, wo_h, conv_gain, cw,
           out, x, wq, wk, wv, wo, side, normed, q2, kb, vb, ka, va, att, hid, act, wf,
           load, s1, s2, s3, ra, sp, rp, sw1, rw1, sw2, rw2, sh, rh):
    v, j = lax.axis_index("view"), lax.axis_index("tm")
    nf, tok, width = x.shape
    part = tok // pieces
    shard = cw.shape[0]
    groups = nt // 2
    a, b = j // 2, lax.rem(j, 2)
    sibling = a * 2 + 1 - b
    anc, prev = side.at[0], side.at[1]
    root = (v == 0) & (j == 0)
    holder = (j < pieces) & jnp.logical_not(root)
    other = lax.rem(j + 1, nt)

    loads = [
        pltpu.make_async_copy(fr.at[0], x, load.at[0]),
        pltpu.make_async_copy(wq_h, wq, load.at[1]),
        pltpu.make_async_copy(wk_h, wk, load.at[2]),
        pltpu.make_async_copy(wv_h, wv, load.at[3]),
        pltpu.make_async_copy(wo_h, wo, load.at[4]),
    ]
    for c in loads:
        c.start()
    if gather:
        own_rows = pl.ds(pl.multiple_of(j * shard, 16), shard)
        own_w = pltpu.make_async_copy(cw, wf.at[own_rows], load.at[5])
    else:
        own_w = pltpu.make_async_copy(cw, wf, load.at[5])
    own_w.start()

    barrier = pltpu.get_barrier_semaphore()

    @pl.loop(0, nt)
    def _(t):
        @pl.when(t != j)
        def _():
            pl.semaphore_signal(barrier, inc=1, device_id=(v, t), device_id_type=MESH)

    @pl.loop(0, nv)
    def _(t):
        @pl.when(t != v)
        def _():
            pl.semaphore_signal(barrier, inc=1, device_id=(t, j), device_id_type=MESH)

    pl.semaphore_wait(barrier, nt - 1 + nv - 1)

    def rows(p):
        return pl.ds(pl.multiple_of(p * part, part), part)

    def spread(p, src, act_on):
        @pl.when(v == 0)
        def _():
            @pl.loop(1, nv)
            def _(t):
                act_on(remote(src, anc.at[rows(p)], s2.at[t], ra.at[p], t, j))

        @pl.loop(0, nt)
        def _(t):
            @pl.when((t != j) & ((v != 0) | (t != 0)))
            def _():
                act_on(remote(src, anc.at[rows(p)], s3.at[t], ra.at[p], v, t))

    def scatter(act_on):
        @pl.loop(1, pieces)
        def _(p):
            act_on(remote(fr.at[0, 0, rows(p)], anc.at[rows(p)], s1.at[p], ra.at[p], 0, p))

    def begin(c):
        c.start()

    def sent(c):
        c.wait_send()

    def landed(p):
        remote(anc.at[rows(p)], anc.at[rows(p)], s1.at[p], ra.at[p], v, other).wait_recv()

    def forward():
        landed(j)
        spread(j, anc.at[rows(j)], begin)

    own_anchor = pltpu.make_async_copy(fr.at[0, 0], anc, load.at[6])
    own_prev = pltpu.make_async_copy(fr.at[0, 0], prev, load.at[7])
    to_next = remote(fr.at[0, nf - 1], prev, sp, rp, v, other)

    @pl.when(root)
    def _():
        scatter(begin)
        spread(0, fr.at[0, 0, rows(0)], begin)
        own_anchor.start()

    @pl.when(j < nt - 1)
    def _():
        to_next.start()

    @pl.when(j == 0)
    def _():
        own_prev.start()

    gain = ln_gain[...].reshape(1, width)
    loads[0].wait()

    @pl.loop(0, nf)
    def _(f):
        normed[pl.ds(pl.multiple_of(f * tok, tok), tok), :] = layer_norm(x[f].astype(F32), gain).astype(BF16)

    @pl.when(holder & (v == 0))
    def _():
        forward()

    def across(act_on):
        @pl.loop(1, groups)
        def _(d):
            t = lax.rem(a + groups - d, groups)
            act_on(remote(cw, wf.at[own_rows], sw1.at[t], rw1.at[a], v, t * 2 + b))

    def shard_rows(t, side_of):
        return pl.ds(pl.multiple_of((t * 2 + side_of) * shard, 16), shard)

    def to_sibling(t):
        return remote(wf.at[shard_rows(t, b)], wf.at[shard_rows(t, b)], sw2.at[t], rw2.at[t], v, sibling)

    if gather:
        across(begin)
        own_w.wait()
        to_sibling(a).start()

    lane = lax.broadcasted_iota(jnp.int32, (1, width), 1)
    low = jnp.where(lax.rem(lane, PAIR) < HEAD_DIM, 1.0, 0.0).astype(F32)
    loads[1].wait()
    query = mm(normed[...], wq[...]) * HEAD_DIM ** (-0.5)
    for f in range(nf):
        block = query[f * tok:(f + 1) * tok]
        q2[f, 0:tok, :] = (block * low).astype(BF16)
        q2[f, tok:2 * tok, :] = (block * (1.0 - low)).astype(BF16)
    loads[2].wait()
    loads[3].wait()
    if nf > 1:
        inner = (nf - 1) * tok
        kb[tok:nf * tok, :] = mm(normed[0:inner, :], wk[...]).astype(BF16)
        vb[tok:nf * tok, :] = mm(normed[0:inner, :], wv[...]).astype(BF16)

    @pl.when(holder & (v != 0))
    def _():
        forward()

    @pl.when(j == 0)
    def _():
        own_prev.wait()

    @pl.when(j > 0)
    def _():
        to_next.wait_recv()

    @pl.when(root)
    def _():
        own_anchor.wait()

    @pl.when(jnp.logical_not(root))
    def _():
        @pl.loop(0, pieces)
        def _(p):
            @pl.when(p != j)
            def _():
                landed(p)

    sides = layer_norm(side[...].astype(F32).reshape(2 * tok, width), gain).astype(BF16)
    keys = mm(sides, wk[...]).astype(BF16)
    values = mm(sides, wv[...]).astype(BF16)
    ka[...] = keys[0:tok]
    va[...] = values[0:tok]
    kb[0:tok, :] = keys[tok:2 * tok]
    vb[0:tok, :] = values[tok:2 * tok]

    loads[4].wait()
    c_gain = conv_gain[...].reshape(1, width)
    ones = jnp.ones((2 * tok, PAIR), BF16)
    first_half = lax.broadcasted_iota(jnp.int32, (1, PAIR), 1) < HEAD_DIM
    to_right = remote(act.at[pl.ds(nf * tok, tok)], act.at[pl.ds(0, tok)], sh.at[0], rh.at[0], v, other)
    left = lax.rem(j + nt - 1, nt)
    to_left = remote(act.at[pl.ds(tok, tok)], act.at[pl.ds((nf + 1) * tok, tok)], sh.at[1], rh.at[1], v, left)

    @pl.loop(0, nf)
    def _(i):
        f = lax.rem(i + nf - 1, nf)
        if gather:
            @pl.loop(1, groups)
            def _(d):
                @pl.when(i == d * nf // groups)
                def _():
                    t = lax.rem(a + d, groups)
                    remote(cw, wf.at[shard_rows(t, b)], sw1.at[t], rw1.at[t], v, other).wait_recv()
                    to_sibling(t).start()

        frame = pl.ds(pl.multiple_of(f * tok, tok), tok)
        for h in range(width // PAIR):
            cols = slice(h * PAIR, (h + 1) * PAIR)
            keyset = jnp.concatenate([ka[:, cols], kb[frame, cols]], axis=0)
            valueset = jnp.concatenate([va[:, cols], vb[frame, cols]], axis=0)
            scores = lax.dot_general(
                q2[f, :, cols], keyset, (((1,), (1,)), ((), ())), preferred_element_type=F32
            )
            expo = jnp.exp(scores - jnp.max(scores, axis=-1, keepdims=True))
            summed = mm(expo.astype(BF16), jnp.concatenate([valueset, ones], axis=1))
            mixed = summed[:, 0:PAIR] / summed[:, PAIR:2 * PAIR]
            att[:, cols] = jnp.where(first_half, mixed[0:tok], mixed[tok:2 * tok]).astype(BF16)
        hidden = (x[f].astype(F32) + mm(att[...], wo[...])).astype(BF16)
        hid[frame, :] = hidden
        normal = layer_norm(hidden.astype(F32), c_gain)
        act[pl.ds(pl.multiple_of((f + 1) * tok, tok), tok), :] = (normal * jax.nn.sigmoid(normal)).astype(BF16)

        @pl.when((i == 0) & (j < nt - 1))
        def _():
            to_right.start()

        @pl.when((f == 0) & (j > 0))
        def _():
            to_left.start()

    @pl.when(j == 0)
    def _():
        act[0:tok, :] = jnp.zeros((tok, width), BF16)

    @pl.when(j > 0)
    def _():
        to_right.wait_recv()

    @pl.when(j == nt - 1)
    def _():
        act[(nf + 1) * tok:(nf + 2) * tok, :] = jnp.zeros((tok, width), BF16)

    @pl.when(j < nt - 1)
    def _():
        to_left.wait_recv()

    if gather:
        @pl.loop(0, groups)
        def _(t):
            remote(cw, wf.at[shard_rows(t, 1 - b)], sw2.at[t], rw2.at[t], v, other).wait_recv()
    else:
        own_w.wait()

    total = hid[...].astype(F32)
    for tap in range(3):
        total += mm(act[tap * tok:(tap + nf) * tok, :], wf[tap * width:(tap + 1) * width, :])
    out[...] = total.astype(BF16).reshape(out.shape)

    @pl.when(root)
    def _():
        scatter(sent)
        spread(0, fr.at[0, 0, rows(0)], sent)

    @pl.when(holder)
    def _():
        spread(j, anc.at[rows(j)], sent)

    @pl.when(j < nt - 1)
    def _():
        to_next.wait_send()
        to_right.wait_send()

    @pl.when(j > 0)
    def _():
        to_left.wait_send()

    if gather:
        across(sent)

        @pl.loop(0, groups)
        def _(t):
            to_sibling(t).wait_send()


def hand_over(src, out, done):
    copies = [pltpu.make_async_copy(src.at[0, f], out.at[0, f], done.at[f]) for f in range(src.shape[1])]
    for c in copies:
        c.start()
    for c in copies:
        c.wait()


def solution(mesh):
    nv, nt = mesh.shape["view"], mesh.shape["tm"]

    def per_device(frames, ln_gain, w_query, w_key, w_value, w_out, conv_gain, conv_weight):
        _, nf, tok, width = frames.shape
        shard = conv_weight.shape[0]
        gather = nt % 2 == 0 and shard % 16 == 0
        if not gather:
            conv_weight = lax.all_gather(conv_weight, "tm", axis=0, tiled=True)
        pieces = max(n for n in range(1, nt + 1) if tok % (16 * n) == 0)
        anywhere = pl.BlockSpec(memory_space=pltpu.HBM)
        vmem = pl.BlockSpec(memory_space=pltpu.VMEM)
        square = pltpu.VMEM((width, width), BF16)
        dma = pltpu.SemaphoreType.DMA
        block = pl.pallas_call(
            functools.partial(kernel, nv, nt, pieces, gather),
            out_shape=pltpu.VMEM(frames.shape, BF16),
            in_specs=[anywhere, vmem, anywhere, anywhere, anywhere, anywhere, vmem, anywhere],
            out_specs=vmem,
            scratch_shapes=[
                pltpu.VMEM((nf, tok, width), BF16),
                square, square, square, square,
                pltpu.VMEM((2, tok, width), BF16),
                pltpu.VMEM((nf * tok, width), BF16),
                pltpu.VMEM((nf, 2 * tok, width), BF16),
                pltpu.VMEM((nf * tok, width), BF16),
                pltpu.VMEM((nf * tok, width), BF16),
                pltpu.VMEM((tok, width), BF16),
                pltpu.VMEM((tok, width), BF16),
                pltpu.VMEM((tok, width), BF16),
                pltpu.VMEM((nf * tok, width), BF16),
                pltpu.VMEM(((nf + 2) * tok, width), BF16),
                pltpu.VMEM((3 * width, width), BF16),
                dma((8,)), dma((pieces,)), dma((nv,)), dma((nt,)), dma((pieces,)),
                dma, dma,
                dma((nt,)), dma((nt,)), dma((nt,)), dma((nt,)), dma((2,)), dma((2,)),
            ],
            compiler_params=pltpu.CompilerParams(
                collective_id=0, has_side_effects=True, vmem_limit_bytes=48 * 1024 * 1024
            ),
        )(frames, ln_gain, w_query, w_key, w_value, w_out, conv_gain, conv_weight)
        return pl.pallas_call(
            hand_over,
            out_shape=jax.ShapeDtypeStruct(frames.shape, BF16),
            in_specs=[vmem],
            out_specs=anywhere,
            scratch_shapes=[dma((nf,))],
        )(block)

    placed = (P("view", "tm", None, None), P(), P(), P(), P(), P(), P(), P("tm", None))
    return jax.shard_map(
        per_device, mesh=mesh, in_specs=placed, out_specs=P("view", "tm", None, None), check_vma=False
    )
```

```python
import functools

import jax
import jax.numpy as jnp
from jax import lax
from jax.experimental import pallas as pl
from jax.experimental.pallas import tpu as pltpu
from jax.sharding import PartitionSpec as P

HEAD_DIM = 64
PAIR = 2 * HEAD_DIM
MESH = pl.DeviceIdType.MESH
F32, BF16 = jnp.float32, jnp.bfloat16


def layer_norm(values, gain):
    mean = jnp.mean(values, axis=-1, keepdims=True)
    centred = values - mean
    variance = jnp.mean(centred * centred, axis=-1, keepdims=True)
    return centred * lax.rsqrt(variance + 1e-05) * gain


def mm(a, b):
    return jnp.dot(a, b, preferred_element_type=F32)


def remote(src, dst, send, recv, view, tm):
    return pltpu.make_async_remote_copy(
        src_ref=src, dst_ref=dst, send_sem=send, recv_sem=recv, device_id=(view, tm), device_id_type=MESH
    )


def kernel(nv, nt, pieces, gather,
           fr, ln_gain_h, wq_h, wk_h, wv_h, wo_h, conv_gain_h, cw,
           out, x, wq, wk, wv, wo, side, normed, q2, kb, vb, ka, va, att, hid, act, wf, ln_gain, conv_gain,
           load, s1, s3, ra, sp, rp, sw1, rw1, sw2, rw2, sh, rh):
    v, j = lax.axis_index("view"), lax.axis_index("tm")
    nf, tok, width = x.shape
    part = tok // pieces
    shard = cw.shape[0]
    groups = nt // 2
    a, b = j // 2, lax.rem(j, 2)
    sibling = a * 2 + 1 - b
    anc, prev = side.at[0], side.at[1]
    root = (v == 0) & (j == 0)
    holder = (j < pieces) & jnp.logical_not(root)
    other = lax.rem(j + 1, nt)

    loads = [
        pltpu.make_async_copy(fr.at[0], x, load.at[0]),
        pltpu.make_async_copy(wq_h, wq, load.at[1]),
        pltpu.make_async_copy(wk_h, wk, load.at[2]),
        pltpu.make_async_copy(wv_h, wv, load.at[3]),
        pltpu.make_async_copy(wo_h, wo, load.at[4]),
        pltpu.make_async_copy(ln_gain_h, ln_gain, load.at[8]),
        pltpu.make_async_copy(conv_gain_h, conv_gain, load.at[9]),
    ]
    for c in loads:
        c.start()
    if gather:
        own_rows = pl.ds(pl.multiple_of(j * shard, 16), shard)
        own_w = pltpu.make_async_copy(cw, wf.at[own_rows], load.at[5])
    else:
        own_w = pltpu.make_async_copy(cw, wf, load.at[5])
    own_w.start()

    barrier = pltpu.get_barrier_semaphore()

    @pl.loop(0, nt)
    def _(t):
        @pl.when(t != j)
        def _():
            pl.semaphore_signal(barrier, inc=1, device_id=(v, t), device_id_type=MESH)

    @pl.when((v > 0) & (j < pieces))
    def _():
        pl.semaphore_signal(barrier, inc=1, device_id=(0, 0), device_id_type=MESH)

    @pl.when(root)
    def _():
        @pl.loop(1, nv)
        def _(t):
            @pl.loop(0, pieces)
            def _(p):
                pl.semaphore_signal(barrier, inc=1, device_id=(t, p), device_id_type=MESH)

    far_holder = (v > 0) & (j < pieces)

    @pl.when(root)
    def _():
        pl.semaphore_wait(barrier, nt - 1 + (nv - 1) * pieces)

    @pl.when(far_holder)
    def _():
        pl.semaphore_wait(barrier, nt)

    @pl.when(jnp.logical_not(root | far_holder))
    def _():
        pl.semaphore_wait(barrier, nt - 1)

    def rows(p):
        return pl.ds(pl.multiple_of(p * part, part), part)

    def spread(p, src, act_on):
        @pl.loop(0, nt)
        def _(t):
            @pl.when((t != j) & ((v != 0) | (t != 0)))
            def _():
                act_on(remote(src, anc.at[rows(p)], s3.at[t], ra.at[p], v, t))

    def scatter(act_on):
        @pl.loop(0, nv)
        def _(back):
            t = nv - 1 - back

            @pl.loop(0, pieces)
            def _(p):
                @pl.when((t != 0) | (p != 0))
                def _():
                    act_on(remote(fr.at[0, 0, rows(p)], anc.at[rows(p)], s1.at[t, p], ra.at[p], t, p))

    def begin(c):
        c.start()

    def sent(c):
        c.wait_send()

    def landed(p):
        remote(anc.at[rows(p)], anc.at[rows(p)], s3.at[0], ra.at[p], v, other).wait_recv()

    def forward():
        landed(j)
        spread(j, anc.at[rows(j)], begin)

    own_anchor = pltpu.make_async_copy(fr.at[0, 0], anc, load.at[6])
    own_prev = pltpu.make_async_copy(fr.at[0, 0], prev, load.at[7])
    to_next = remote(fr.at[0, nf - 1], prev, sp, rp, v, other)

    @pl.when(root)
    def _():
        scatter(begin)
        spread(0, fr.at[0, 0, rows(0)], begin)
        own_anchor.start()

    @pl.when(j < nt - 1)
    def _():
        to_next.start()

    @pl.when(j == 0)
    def _():
        own_prev.start()

    loads[0].wait()
    loads[5].wait()
    gain = ln_gain[...].reshape(1, width)

    @pl.loop(0, nf)
    def _(f):
        normed[pl.ds(pl.multiple_of(f * tok, tok), tok), :] = layer_norm(x[f].astype(F32), gain).astype(BF16)

    def across(act_on):
        @pl.loop(1, groups)
        def _(d):
            t = lax.rem(a + groups - d, groups)
            act_on(remote(cw, wf.at[own_rows], sw1.at[t], rw1.at[a], v, t * 2 + b))

    def shard_rows(t, side_of):
        return pl.ds(pl.multiple_of((t * 2 + side_of) * shard, 16), shard)

    def to_sibling(t):
        return remote(wf.at[shard_rows(t, b)], wf.at[shard_rows(t, b)], sw2.at[t], rw2.at[t], v, sibling)

    lane = lax.broadcasted_iota(jnp.int32, (1, width), 1)
    low = jnp.where(lax.rem(lane, PAIR) < HEAD_DIM, 1.0, 0.0).astype(F32)
    loads[1].wait()
    query = mm(normed[...], wq[...]) * HEAD_DIM ** (-0.5)
    for f in range(nf):
        block = query[f * tok:(f + 1) * tok]
        q2[f, 0:tok, :] = (block * low).astype(BF16)
        q2[f, tok:2 * tok, :] = (block * (1.0 - low)).astype(BF16)

    @pl.when(holder)
    def _():
        forward()

    if gather:
        across(begin)
        own_w.wait()
        to_sibling(a).start()

    loads[2].wait()
    loads[3].wait()
    if nf > 1:
        inner = (nf - 1) * tok
        kb[tok:nf * tok, :] = mm(normed[0:inner, :], wk[...]).astype(BF16)
        vb[tok:nf * tok, :] = mm(normed[0:inner, :], wv[...]).astype(BF16)

    @pl.when(j == 0)
    def _():
        own_prev.wait()

    @pl.when(j > 0)
    def _():
        to_next.wait_recv()

    def projected(frame):
        frame = layer_norm(frame.astype(F32), gain).astype(BF16)
        return mm(frame, wk[...]).astype(BF16), mm(frame, wv[...]).astype(BF16)

    kb[0:tok, :], vb[0:tok, :] = projected(prev[...])

    @pl.when(root)
    def _():
        own_anchor.wait()

    @pl.when(jnp.logical_not(root))
    def _():
        @pl.loop(0, pieces)
        def _(p):
            @pl.when(p != j)
            def _():
                landed(p)

    ka[...], va[...] = projected(anc[...])

    loads[4].wait()
    loads[6].wait()
    c_gain = conv_gain[...].reshape(1, width)
    ones = jnp.ones((2 * tok, PAIR), BF16)
    first_half = lax.broadcasted_iota(jnp.int32, (1, PAIR), 1) < HEAD_DIM
    to_right = remote(act.at[pl.ds(nf * tok, tok)], act.at[pl.ds(0, tok)], sh.at[0], rh.at[0], v, other)
    left = lax.rem(j + nt - 1, nt)
    to_left = remote(act.at[pl.ds(tok, tok)], act.at[pl.ds((nf + 1) * tok, tok)], sh.at[1], rh.at[1], v, left)

    @pl.loop(0, nf)
    def _(i):
        f = lax.rem(i + nf - 1, nf)
        if gather:
            @pl.loop(1, groups)
            def _(d):
                @pl.when(i == d * nf // groups)
                def _():
                    t = lax.rem(a + d, groups)
                    remote(cw, wf.at[shard_rows(t, b)], sw1.at[t], rw1.at[t], v, other).wait_recv()
                    to_sibling(t).start()

        frame = pl.ds(pl.multiple_of(f * tok, tok), tok)
        for h in range(width // PAIR):
            cols = slice(h * PAIR, (h + 1) * PAIR)
            keyset = jnp.concatenate([ka[:, cols], kb[frame, cols]], axis=0)
            valueset = jnp.concatenate([va[:, cols], vb[frame, cols]], axis=0)
            scores = lax.dot_general(
                q2[f, :, cols], keyset, (((1,), (1,)), ((), ())), preferred_element_type=F32
            )
            expo = jnp.exp(scores - jnp.max(scores, axis=-1, keepdims=True))
            summed = mm(expo.astype(BF16), jnp.concatenate([valueset, ones], axis=1))
            mixed = summed[:, 0:PAIR] / summed[:, PAIR:2 * PAIR]
            att[:, cols] = jnp.where(first_half, mixed[0:tok], mixed[tok:2 * tok]).astype(BF16)
        hidden = (x[f].astype(F32) + mm(att[...], wo[...])).astype(BF16)
        hid[frame, :] = hidden
        normal = layer_norm(hidden.astype(F32), c_gain)
        act[pl.ds(pl.multiple_of((f + 1) * tok, tok), tok), :] = (normal * jax.nn.sigmoid(normal)).astype(BF16)

        @pl.when((i == 0) & (j < nt - 1))
        def _():
            to_right.start()

        @pl.when((f == 0) & (j > 0))
        def _():
            to_left.start()

    @pl.when(j == 0)
    def _():
        act[0:tok, :] = jnp.zeros((tok, width), BF16)

    @pl.when(j > 0)
    def _():
        to_right.wait_recv()

    @pl.when(j == nt - 1)
    def _():
        act[(nf + 1) * tok:(nf + 2) * tok, :] = jnp.zeros((tok, width), BF16)

    @pl.when(j < nt - 1)
    def _():
        to_left.wait_recv()

    if gather:
        @pl.loop(0, groups)
        def _(t):
            remote(cw, wf.at[shard_rows(t, 1 - b)], sw2.at[t], rw2.at[t], v, other).wait_recv()
    else:
        own_w.wait()

    total = hid[...].astype(F32)
    for tap in range(3):
        total += mm(act[tap * tok:(tap + nf) * tok, :], wf[tap * width:(tap + 1) * width, :])
    out[...] = total.astype(BF16).reshape(out.shape)

    @pl.when(root)
    def _():
        scatter(sent)
        spread(0, fr.at[0, 0, rows(0)], sent)

    @pl.when(holder)
    def _():
        spread(j, anc.at[rows(j)], sent)

    @pl.when(j < nt - 1)
    def _():
        to_next.wait_send()
        to_right.wait_send()

    @pl.when(j > 0)
    def _():
        to_left.wait_send()

    if gather:
        across(sent)

        @pl.loop(0, groups)
        def _(t):
            to_sibling(t).wait_send()


def solution(mesh):
    nv, nt = mesh.shape["view"], mesh.shape["tm"]

    def per_device(frames, ln_gain, w_query, w_key, w_value, w_out, conv_gain, conv_weight):
        _, nf, tok, width = frames.shape
        shard = conv_weight.shape[0]
        gather = nt % 2 == 0 and shard % 16 == 0
        if not gather:
            conv_weight = lax.all_gather(conv_weight, "tm", axis=0, tiled=True)
        pieces = max(n for n in range(1, nt + 1) if tok % (16 * n) == 0)
        anywhere = pl.BlockSpec(memory_space=pl.ANY)
        vmem = pl.BlockSpec(memory_space=pltpu.VMEM)
        square = pltpu.VMEM((width, width), BF16)
        dma = pltpu.SemaphoreType.DMA
        return pl.pallas_call(
            functools.partial(kernel, nv, nt, pieces, gather),
            out_shape=jax.ShapeDtypeStruct(frames.shape, BF16),
            in_specs=[anywhere] * 8,
            out_specs=vmem,
            scratch_shapes=[
                pltpu.VMEM((nf, tok, width), BF16),
                square, square, square, square,
                pltpu.VMEM((2, tok, width), BF16),
                pltpu.VMEM((nf * tok, width), BF16),
                pltpu.VMEM((nf, 2 * tok, width), BF16),
                pltpu.VMEM((nf * tok, width), BF16),
                pltpu.VMEM((nf * tok, width), BF16),
                pltpu.VMEM((tok, width), BF16),
                pltpu.VMEM((tok, width), BF16),
                pltpu.VMEM((tok, width), BF16),
                pltpu.VMEM((nf * tok, width), BF16),
                pltpu.VMEM(((nf + 2) * tok, width), BF16),
                pltpu.VMEM((3 * width, width), BF16),
                pltpu.VMEM((width,), F32),
                pltpu.VMEM((width,), F32),
                dma((10,)), dma((nv, pieces)), dma((nt,)), dma((pieces,)),
                dma, dma,
                dma((nt,)), dma((nt,)), dma((nt,)), dma((nt,)), dma((2,)), dma((2,)),
            ],
            compiler_params=pltpu.CompilerParams(
                collective_id=0, has_side_effects=True, vmem_limit_bytes=62 * 1024 * 1024
            ),
        )(frames, ln_gain, w_query, w_key, w_value, w_out, conv_gain, conv_weight)
    placed = (P("view", "tm", None, None), P(), P(), P(), P(), P(), P(), P("tm", None))
    return jax.shard_map(
        per_device, mesh=mesh, in_specs=placed, out_specs=P("view", "tm", None, None), check_vma=False
    )
```

```python
import functools

import jax
import jax.numpy as jnp
from jax import lax
from jax.experimental import pallas as pl
from jax.experimental.pallas import tpu as pltpu
from jax.sharding import PartitionSpec as P

HEAD_DIM = 64
PAIR = 2 * HEAD_DIM
MESH = pl.DeviceIdType.MESH
F32, BF16 = jnp.float32, jnp.bfloat16


def layer_norm(values, gain):
    mean = jnp.mean(values, axis=-1, keepdims=True)
    centred = values - mean
    variance = jnp.mean(centred * centred, axis=-1, keepdims=True)
    return centred * lax.rsqrt(variance + 1e-05) * gain


def mm(a, b):
    return jnp.dot(a, b, preferred_element_type=F32)


def remote(src, dst, send, recv, view, tm):
    return pltpu.make_async_remote_copy(
        src_ref=src, dst_ref=dst, send_sem=send, recv_sem=recv, device_id=(view, tm), device_id_type=MESH
    )


def kernel(nv, nt, pieces, gather,
           fr, ln_gain_h, wq_h, wk_h, wv_h, wo_h, conv_gain_h, cw,
           out, x, wq, wk, wv, wo, side, normed, q2, kb, vb, ka, va, att, hid, act, wf, ln_gain, conv_gain,
           load, s1, s2, s3, ra, sp, rp, sw1, rw1, sw2, rw2, sh, rh):
    v, j = lax.axis_index("view"), lax.axis_index("tm")
    nf, tok, width = x.shape
    part = tok // pieces
    shard = cw.shape[0]
    groups = nt // 2
    a, b = j // 2, lax.rem(j, 2)
    sibling = a * 2 + 1 - b
    anc, prev = side.at[0], side.at[1]
    root = (v == 0) & (j == 0)
    holder = (j < pieces) & jnp.logical_not(root)
    other = lax.rem(j + 1, nt)

    loads = [
        pltpu.make_async_copy(fr.at[0], x, load.at[0]),
        pltpu.make_async_copy(wq_h, wq, load.at[1]),
        pltpu.make_async_copy(wk_h, wk, load.at[2]),
        pltpu.make_async_copy(wv_h, wv, load.at[3]),
        pltpu.make_async_copy(wo_h, wo, load.at[4]),
        pltpu.make_async_copy(ln_gain_h, ln_gain, load.at[8]),
        pltpu.make_async_copy(conv_gain_h, conv_gain, load.at[9]),
    ]
    for c in loads:
        c.start()
    if gather:
        own_rows = pl.ds(pl.multiple_of(j * shard, 16), shard)
        own_w = pltpu.make_async_copy(cw, wf.at[own_rows], load.at[5])
    else:
        own_w = pltpu.make_async_copy(cw, wf, load.at[5])
    own_w.start()

    barrier = pltpu.get_barrier_semaphore()

    @pl.loop(0, nt)
    def _(t):
        @pl.when(t != j)
        def _():
            pl.semaphore_signal(barrier, inc=1, device_id=(v, t), device_id_type=MESH)

    @pl.when(j < pieces)
    def _():
        @pl.loop(0, nv)
        def _(t):
            @pl.when(t != v)
            def _():
                pl.semaphore_signal(barrier, inc=1, device_id=(t, j), device_id_type=MESH)

        pl.semaphore_wait(barrier, nt - 1 + nv - 1)

    @pl.when(j >= pieces)
    def _():
        pl.semaphore_wait(barrier, nt - 1)

    def rows(p):
        return pl.ds(pl.multiple_of(p * part, part), part)

    def spread(p, src, act_on):
        @pl.when(v == 0)
        def _():
            @pl.loop(1, nv)
            def _(back):
                t = nv - back
                act_on(remote(src, anc.at[rows(p)], s2.at[t], ra.at[p], t, j))

        @pl.loop(0, nt)
        def _(t):
            @pl.when((t != j) & ((v != 0) | (t != 0)))
            def _():
                act_on(remote(src, anc.at[rows(p)], s3.at[t], ra.at[p], v, t))

    def scatter(act_on):
        @pl.loop(1, pieces)
        def _(p):
            act_on(remote(fr.at[0, 0, rows(p)], anc.at[rows(p)], s1.at[p], ra.at[p], 0, p))

    def begin(c):
        c.start()

    def sent(c):
        c.wait_send()

    def landed(p):
        remote(anc.at[rows(p)], anc.at[rows(p)], s3.at[0], ra.at[p], v, other).wait_recv()

    def forward():
        landed(j)
        spread(j, anc.at[rows(j)], begin)

    own_anchor = pltpu.make_async_copy(fr.at[0, 0], anc, load.at[6])
    own_prev = pltpu.make_async_copy(fr.at[0, 0], prev, load.at[7])
    to_next = remote(fr.at[0, nf - 1], prev, sp, rp, v, other)

    @pl.when(root)
    def _():
        scatter(begin)
        spread(0, fr.at[0, 0, rows(0)], begin)
        own_anchor.start()

    @pl.when(j < nt - 1)
    def _():
        to_next.start()

    @pl.when(j == 0)
    def _():
        own_prev.start()

    loads[0].wait()
    loads[5].wait()
    gain = ln_gain[...].reshape(1, width)

    @pl.when(holder & (v == 0))
    def _():
        forward()

    @pl.loop(0, nf)
    def _(f):
        normed[pl.ds(pl.multiple_of(f * tok, tok), tok), :] = layer_norm(x[f].astype(F32), gain).astype(BF16)

    def across(act_on):
        @pl.loop(1, groups)
        def _(d):
            t = lax.rem(a + groups - d, groups)
            act_on(remote(cw, wf.at[own_rows], sw1.at[t], rw1.at[a], v, t * 2 + b))

    def shard_rows(t, side_of):
        return pl.ds(pl.multiple_of((t * 2 + side_of) * shard, 16), shard)

    def to_sibling(t):
        return remote(wf.at[shard_rows(t, b)], wf.at[shard_rows(t, b)], sw2.at[t], rw2.at[t], v, sibling)

    lane = lax.broadcasted_iota(jnp.int32, (1, width), 1)
    low = jnp.where(lax.rem(lane, PAIR) < HEAD_DIM, 1.0, 0.0).astype(F32)
    loads[1].wait()
    query = mm(normed[...], wq[...]) * HEAD_DIM ** (-0.5)
    for f in range(nf):
        block = query[f * tok:(f + 1) * tok]
        q2[f, 0:tok, :] = (block * low).astype(BF16)
        q2[f, tok:2 * tok, :] = (block * (1.0 - low)).astype(BF16)

    @pl.when(holder & (v != 0))
    def _():
        forward()

    if gather:
        across(begin)
        own_w.wait()
        to_sibling(a).start()

    loads[2].wait()
    loads[3].wait()
    if nf > 1:
        inner = (nf - 1) * tok
        kb[tok:nf * tok, :] = mm(normed[0:inner, :], wk[...]).astype(BF16)
        vb[tok:nf * tok, :] = mm(normed[0:inner, :], wv[...]).astype(BF16)

    @pl.when(j == 0)
    def _():
        own_prev.wait()

    @pl.when(j > 0)
    def _():
        to_next.wait_recv()

    def projected(frame):
        frame = layer_norm(frame.astype(F32), gain).astype(BF16)
        return mm(frame, wk[...]).astype(BF16), mm(frame, wv[...]).astype(BF16)

    kb[0:tok, :], vb[0:tok, :] = projected(prev[...])

    @pl.when(root)
    def _():
        own_anchor.wait()

    @pl.when(jnp.logical_not(root))
    def _():
        @pl.loop(0, pieces)
        def _(p):
            @pl.when(p != j)
            def _():
                landed(p)

    ka[...], va[...] = projected(anc[...])

    loads[4].wait()
    loads[6].wait()
    c_gain = conv_gain[...].reshape(1, width)
    ones = jnp.ones((2 * tok, PAIR), BF16)
    first_half = lax.broadcasted_iota(jnp.int32, (1, PAIR), 1) < HEAD_DIM
    to_right = remote(act.at[pl.ds(nf * tok, tok)], act.at[pl.ds(0, tok)], sh.at[0], rh.at[0], v, other)
    left = lax.rem(j + nt - 1, nt)
    to_left = remote(act.at[pl.ds(tok, tok)], act.at[pl.ds((nf + 1) * tok, tok)], sh.at[1], rh.at[1], v, left)

    @pl.loop(0, nf)
    def _(i):
        f = lax.rem(i + nf - 1, nf)
        if gather:
            @pl.loop(1, groups)
            def _(d):
                @pl.when(i == d * nf // groups)
                def _():
                    t = lax.rem(a + d, groups)
                    remote(cw, wf.at[shard_rows(t, b)], sw1.at[t], rw1.at[t], v, other).wait_recv()
                    to_sibling(t).start()

        frame = pl.ds(pl.multiple_of(f * tok, tok), tok)
        for h in range(width // PAIR):
            cols = slice(h * PAIR, (h + 1) * PAIR)
            keyset = jnp.concatenate([ka[:, cols], kb[frame, cols]], axis=0)
            valueset = jnp.concatenate([va[:, cols], vb[frame, cols]], axis=0)
            scores = lax.dot_general(
                q2[f, :, cols], keyset, (((1,), (1,)), ((), ())), preferred_element_type=F32
            )
            expo = jnp.exp(scores - jnp.max(scores, axis=-1, keepdims=True))
            summed = mm(expo.astype(BF16), jnp.concatenate([valueset, ones], axis=1))
            mixed = summed[:, 0:PAIR] / summed[:, PAIR:2 * PAIR]
            att[:, cols] = jnp.where(first_half, mixed[0:tok], mixed[tok:2 * tok]).astype(BF16)
        hidden = (x[f].astype(F32) + mm(att[...], wo[...])).astype(BF16)
        hid[frame, :] = hidden
        normal = layer_norm(hidden.astype(F32), c_gain)
        act[pl.ds(pl.multiple_of((f + 1) * tok, tok), tok), :] = (normal * jax.nn.sigmoid(normal)).astype(BF16)

        @pl.when((i == 0) & (j < nt - 1))
        def _():
            to_right.start()

        @pl.when((f == 0) & (j > 0))
        def _():
            to_left.start()

    @pl.when(j == 0)
    def _():
        act[0:tok, :] = jnp.zeros((tok, width), BF16)

    @pl.when(j > 0)
    def _():
        to_right.wait_recv()

    @pl.when(j == nt - 1)
    def _():
        act[(nf + 1) * tok:(nf + 2) * tok, :] = jnp.zeros((tok, width), BF16)

    @pl.when(j < nt - 1)
    def _():
        to_left.wait_recv()

    if gather:
        @pl.loop(0, groups)
        def _(t):
            remote(cw, wf.at[shard_rows(t, 1 - b)], sw2.at[t], rw2.at[t], v, other).wait_recv()
    else:
        own_w.wait()

    total = hid[...].astype(F32)
    for tap in range(3):
        total += mm(act[tap * tok:(tap + nf) * tok, :], wf[tap * width:(tap + 1) * width, :])
    out[...] = total.astype(BF16).reshape(out.shape)

    @pl.when(root)
    def _():
        scatter(sent)
        spread(0, fr.at[0, 0, rows(0)], sent)

    @pl.when(holder)
    def _():
        spread(j, anc.at[rows(j)], sent)

    @pl.when(j < nt - 1)
    def _():
        to_next.wait_send()
        to_right.wait_send()

    @pl.when(j > 0)
    def _():
        to_left.wait_send()

    if gather:
        across(sent)

        @pl.loop(0, groups)
        def _(t):
            to_sibling(t).wait_send()


def solution(mesh):
    nv, nt = mesh.shape["view"], mesh.shape["tm"]

    def per_device(frames, ln_gain, w_query, w_key, w_value, w_out, conv_gain, conv_weight):
        _, nf, tok, width = frames.shape
        shard = conv_weight.shape[0]
        gather = nt % 2 == 0 and shard % 16 == 0
        if not gather:
            conv_weight = lax.all_gather(conv_weight, "tm", axis=0, tiled=True)
        pieces = max(n for n in range(1, nt + 1) if tok % (16 * n) == 0)
        anywhere = pl.BlockSpec(memory_space=pl.ANY)
        vmem = pl.BlockSpec(memory_space=pltpu.VMEM)
        square = pltpu.VMEM((width, width), BF16)
        dma = pltpu.SemaphoreType.DMA
        return pl.pallas_call(
            functools.partial(kernel, nv, nt, pieces, gather),
            out_shape=jax.ShapeDtypeStruct(frames.shape, BF16),
            in_specs=[anywhere] * 8,
            out_specs=vmem,
            scratch_shapes=[
                pltpu.VMEM((nf, tok, width), BF16),
                square, square, square, square,
                pltpu.VMEM((2, tok, width), BF16),
                pltpu.VMEM((nf * tok, width), BF16),
                pltpu.VMEM((nf, 2 * tok, width), BF16),
                pltpu.VMEM((nf * tok, width), BF16),
                pltpu.VMEM((nf * tok, width), BF16),
                pltpu.VMEM((tok, width), BF16),
                pltpu.VMEM((tok, width), BF16),
                pltpu.VMEM((tok, width), BF16),
                pltpu.VMEM((nf * tok, width), BF16),
                pltpu.VMEM(((nf + 2) * tok, width), BF16),
                pltpu.VMEM((3 * width, width), BF16),
                pltpu.VMEM((width,), F32),
                pltpu.VMEM((width,), F32),
                dma((10,)), dma((pieces,)), dma((nv,)), dma((nt,)), dma((pieces,)),
                dma, dma,
                dma((nt,)), dma((nt,)), dma((nt,)), dma((nt,)), dma((2,)), dma((2,)),
            ],
            compiler_params=pltpu.CompilerParams(
                collective_id=0, has_side_effects=True, vmem_limit_bytes=62 * 1024 * 1024
            ),
        )(frames, ln_gain, w_query, w_key, w_value, w_out, conv_gain, conv_weight)
    placed = (P("view", "tm", None, None), P(), P(), P(), P(), P(), P(), P("tm", None))
    return jax.shard_map(
        per_device, mesh=mesh, in_specs=placed, out_specs=P("view", "tm", None, None), check_vma=False
    )
```

```python
import functools

import jax
import jax.numpy as jnp
from jax import lax
from jax.experimental import pallas as pl
from jax.experimental.pallas import tpu as pltpu
from jax.sharding import PartitionSpec as P

HEAD_DIM = 64
PAIR = 2 * HEAD_DIM
MESH = pl.DeviceIdType.MESH
F32, BF16 = jnp.float32, jnp.bfloat16


def layer_norm(values, gain):
    mean = jnp.mean(values, axis=-1, keepdims=True)
    centred = values - mean
    variance = jnp.mean(centred * centred, axis=-1, keepdims=True)
    return centred * lax.rsqrt(variance + 1e-05) * gain


def mm(a, b):
    return jnp.dot(a, b, preferred_element_type=F32)


def remote(src, dst, send, recv, view, tm):
    return pltpu.make_async_remote_copy(
        src_ref=src, dst_ref=dst, send_sem=send, recv_sem=recv, device_id=(view, tm), device_id_type=MESH
    )


def kernel(nv, nt, pieces, gather,
           fr, ln_gain_h, wq_h, wk_h, wv_h, wo_h, conv_gain_h, cw,
           out, x, wq, wk, wv, wo, side, normed, q2, kb, vb, ka, va, att, hid, act, wf, ln_gain, conv_gain,
           load, s1, s2, s3, ra, sp, rp, sw1, rw1, sw2, rw2, sh, rh):
    v, j = lax.axis_index("view"), lax.axis_index("tm")
    nf, tok, width = x.shape
    part = tok // pieces
    shard = cw.shape[0]
    groups = nt // 2
    a, b = j // 2, lax.rem(j, 2)
    sibling = a * 2 + 1 - b
    anc, prev = side.at[0], side.at[1]
    root = (v == 0) & (j == 0)
    holder = (j < pieces) & jnp.logical_not(root)
    other = lax.rem(j + 1, nt)

    loads = [
        pltpu.make_async_copy(fr.at[0], x, load.at[0]),
        pltpu.make_async_copy(wq_h, wq, load.at[1]),
        pltpu.make_async_copy(wk_h, wk, load.at[2]),
        pltpu.make_async_copy(wv_h, wv, load.at[3]),
        pltpu.make_async_copy(wo_h, wo, load.at[4]),
        pltpu.make_async_copy(ln_gain_h, ln_gain, load.at[8]),
        pltpu.make_async_copy(conv_gain_h, conv_gain, load.at[9]),
    ]
    for c in loads:
        c.start()
    if gather:
        own_rows = pl.ds(pl.multiple_of(j * shard, 16), shard)
        own_w = pltpu.make_async_copy(cw, wf.at[own_rows], load.at[5])
    else:
        own_w = pltpu.make_async_copy(cw, wf, load.at[5])
    own_w.start()

    barrier = pltpu.get_barrier_semaphore()

    @pl.loop(0, nt)
    def _(t):
        @pl.when(t != j)
        def _():
            pl.semaphore_signal(barrier, inc=1, device_id=(v, t), device_id_type=MESH)

    @pl.when(j < pieces)
    def _():
        @pl.loop(0, nv)
        def _(t):
            @pl.when(t != v)
            def _():
                pl.semaphore_signal(barrier, inc=1, device_id=(t, j), device_id_type=MESH)

        pl.semaphore_wait(barrier, nt - 1 + nv - 1)

    @pl.when(j >= pieces)
    def _():
        pl.semaphore_wait(barrier, nt - 1)

    def rows(p):
        return pl.ds(pl.multiple_of(p * part, part), part)

    def spread(p, src, act_on):
        @pl.when(v == 0)
        def _():
            @pl.loop(1, nv)
            def _(back):
                t = nv - back
                act_on(remote(src, anc.at[rows(p)], s2.at[t], ra.at[p], t, j))

        @pl.loop(0, nt)
        def _(t):
            @pl.when((t != j) & ((v != 0) | (t != 0)))
            def _():
                act_on(remote(src, anc.at[rows(p)], s3.at[t], ra.at[p], v, t))

    def scatter(act_on):
        @pl.loop(1, pieces)
        def _(p):
            act_on(remote(fr.at[0, 0, rows(p)], anc.at[rows(p)], s1.at[p], ra.at[p], 0, p))

    def begin(c):
        c.start()

    def sent(c):
        c.wait_send()

    def landed(p):
        remote(anc.at[rows(p)], anc.at[rows(p)], s3.at[0], ra.at[p], v, other).wait_recv()

    def forward():
        landed(j)
        spread(j, anc.at[rows(j)], begin)

    own_anchor = pltpu.make_async_copy(fr.at[0, 0], anc, load.at[6])
    own_prev = pltpu.make_async_copy(fr.at[0, 0], prev, load.at[7])
    to_next = remote(fr.at[0, nf - 1], prev, sp, rp, v, other)

    @pl.when(root)
    def _():
        scatter(begin)
        spread(0, fr.at[0, 0, rows(0)], begin)
        own_anchor.start()

    @pl.when(j < nt - 1)
    def _():
        to_next.start()

    @pl.when(j == 0)
    def _():
        own_prev.start()

    loads[0].wait()
    loads[5].wait()
    gain = ln_gain[...].reshape(1, width)

    @pl.when(holder & (v == 0))
    def _():
        forward()

    @pl.loop(0, nf)
    def _(f):
        normed[pl.ds(pl.multiple_of(f * tok, tok), tok), :] = layer_norm(x[f].astype(F32), gain).astype(BF16)

    def across(act_on):
        @pl.loop(1, groups)
        def _(d):
            t = lax.rem(a + groups - d, groups)
            act_on(remote(cw, wf.at[own_rows], sw1.at[t], rw1.at[a], v, t * 2 + b))

    def shard_rows(t, side_of):
        return pl.ds(pl.multiple_of((t * 2 + side_of) * shard, 16), shard)

    def to_sibling(t):
        return remote(wf.at[shard_rows(t, b)], wf.at[shard_rows(t, b)], sw2.at[t], rw2.at[t], v, sibling)

    lane = lax.broadcasted_iota(jnp.int32, (1, width), 1)
    low = jnp.where(lax.rem(lane, PAIR) < HEAD_DIM, 1.0, 0.0).astype(F32)
    loads[1].wait()
    query = mm(normed[...], wq[...]) * HEAD_DIM ** (-0.5)
    for f in range(nf):
        block = query[f * tok:(f + 1) * tok]
        q2[f, 0:tok, :] = (block * low).astype(BF16)
        q2[f, tok:2 * tok, :] = (block * (1.0 - low)).astype(BF16)

    @pl.when(holder & (v != 0))
    def _():
        forward()

    if gather:
        across(begin)
        own_w.wait()
        to_sibling(a).start()

    loads[2].wait()
    loads[3].wait()
    if nf > 1:
        inner = (nf - 1) * tok
        kb[tok:nf * tok, :] = mm(normed[0:inner, :], wk[...]).astype(BF16)
        vb[tok:nf * tok, :] = mm(normed[0:inner, :], wv[...]).astype(BF16)

    @pl.when(j == 0)
    def _():
        own_prev.wait()

    @pl.when(j > 0)
    def _():
        to_next.wait_recv()

    def projected(frame):
        frame = layer_norm(frame.astype(F32), gain).astype(BF16)
        return mm(frame, wk[...]).astype(BF16), mm(frame, wv[...]).astype(BF16)

    kb[0:tok, :], vb[0:tok, :] = projected(prev[...])

    @pl.when(root)
    def _():
        own_anchor.wait()

    @pl.when(jnp.logical_not(root))
    def _():
        @pl.loop(0, pieces)
        def _(p):
            @pl.when(p != j)
            def _():
                landed(p)

    ka[...], va[...] = projected(anc[...])

    loads[4].wait()
    loads[6].wait()
    c_gain = conv_gain[...].reshape(1, width)
    ones = jnp.ones((2 * tok, PAIR), BF16)
    first_half = lax.broadcasted_iota(jnp.int32, (1, PAIR), 1) < HEAD_DIM
    to_right = remote(act.at[pl.ds(nf * tok, tok)], act.at[pl.ds(0, tok)], sh.at[0], rh.at[0], v, other)
    left = lax.rem(j + nt - 1, nt)
    to_left = remote(act.at[pl.ds(tok, tok)], act.at[pl.ds((nf + 1) * tok, tok)], sh.at[1], rh.at[1], v, left)

    @pl.loop(0, nf)
    def _(i):
        f = lax.rem(i + nf - 1, nf)
        if gather:
            @pl.loop(1, groups)
            def _(d):
                @pl.when(i == d * nf // groups)
                def _():
                    t = lax.rem(a + d, groups)
                    remote(cw, wf.at[shard_rows(t, b)], sw1.at[t], rw1.at[t], v, other).wait_recv()
                    to_sibling(t).start()

        frame = pl.ds(pl.multiple_of(f * tok, tok), tok)
        for h in range(width // PAIR):
            cols = slice(h * PAIR, (h + 1) * PAIR)
            keyset = jnp.concatenate([ka[:, cols], kb[frame, cols]], axis=0)
            valueset = jnp.concatenate([va[:, cols], vb[frame, cols]], axis=0)
            scores = lax.dot_general(
                q2[f, :, cols], keyset, (((1,), (1,)), ((), ())), preferred_element_type=F32
            )
            expo = jnp.exp(scores - jnp.max(scores, axis=-1, keepdims=True))
            summed = mm(expo.astype(BF16), jnp.concatenate([valueset, ones], axis=1))
            mixed = summed[:, 0:PAIR] / summed[:, PAIR:2 * PAIR]
            att[:, cols] = jnp.where(first_half, mixed[0:tok], mixed[tok:2 * tok]).astype(BF16)
        hidden = (x[f].astype(F32) + mm(att[...], wo[...])).astype(BF16)
        hid[frame, :] = hidden
        normal = layer_norm(hidden.astype(F32), c_gain)
        act[pl.ds(pl.multiple_of((f + 1) * tok, tok), tok), :] = (normal * jax.nn.sigmoid(normal)).astype(BF16)

        @pl.when((i == 0) & (j < nt - 1))
        def _():
            to_right.start()

        @pl.when((f == 0) & (j > 0))
        def _():
            to_left.start()

    if gather:
        @pl.loop(0, groups)
        def _(t):
            remote(cw, wf.at[shard_rows(t, 1 - b)], sw2.at[t], rw2.at[t], v, other).wait_recv()
    else:
        own_w.wait()

    def tapped(tap):
        return mm(act[tap * tok:(tap + nf) * tok, :], wf[tap * width:(tap + 1) * width, :])

    total = hid[...].astype(F32) + tapped(1)

    @pl.when(j == 0)
    def _():
        act[0:tok, :] = jnp.zeros((tok, width), BF16)

    @pl.when(j > 0)
    def _():
        to_right.wait_recv()

    @pl.when(j == nt - 1)
    def _():
        act[(nf + 1) * tok:(nf + 2) * tok, :] = jnp.zeros((tok, width), BF16)

    @pl.when(j < nt - 1)
    def _():
        to_left.wait_recv()

    total += tapped(0) + tapped(2)
    out[...] = total.astype(BF16).reshape(out.shape)

    @pl.when(root)
    def _():
        scatter(sent)
        spread(0, fr.at[0, 0, rows(0)], sent)

    @pl.when(holder)
    def _():
        spread(j, anc.at[rows(j)], sent)

    @pl.when(j < nt - 1)
    def _():
        to_next.wait_send()
        to_right.wait_send()

    @pl.when(j > 0)
    def _():
        to_left.wait_send()

    if gather:
        across(sent)

        @pl.loop(0, groups)
        def _(t):
            to_sibling(t).wait_send()


def solution(mesh):
    nv, nt = mesh.shape["view"], mesh.shape["tm"]

    def per_device(frames, ln_gain, w_query, w_key, w_value, w_out, conv_gain, conv_weight):
        _, nf, tok, width = frames.shape
        shard = conv_weight.shape[0]
        gather = nt % 2 == 0 and shard % 16 == 0
        if not gather:
            conv_weight = lax.all_gather(conv_weight, "tm", axis=0, tiled=True)
        pieces = max(n for n in range(1, nt + 1) if tok % (16 * n) == 0)
        anywhere = pl.BlockSpec(memory_space=pl.ANY)
        vmem = pl.BlockSpec(memory_space=pltpu.VMEM)
        square = pltpu.VMEM((width, width), BF16)
        dma = pltpu.SemaphoreType.DMA
        return pl.pallas_call(
            functools.partial(kernel, nv, nt, pieces, gather),
            out_shape=jax.ShapeDtypeStruct(frames.shape, BF16),
            in_specs=[anywhere] * 8,
            out_specs=vmem,
            scratch_shapes=[
                pltpu.VMEM((nf, tok, width), BF16),
                square, square, square, square,
                pltpu.VMEM((2, tok, width), BF16),
                pltpu.VMEM((nf * tok, width), BF16),
                pltpu.VMEM((nf, 2 * tok, width), BF16),
                pltpu.VMEM((nf * tok, width), BF16),
                pltpu.VMEM((nf * tok, width), BF16),
                pltpu.VMEM((tok, width), BF16),
                pltpu.VMEM((tok, width), BF16),
                pltpu.VMEM((tok, width), BF16),
                pltpu.VMEM((nf * tok, width), BF16),
                pltpu.VMEM(((nf + 2) * tok, width), BF16),
                pltpu.VMEM((3 * width, width), BF16),
                pltpu.VMEM((width,), F32),
                pltpu.VMEM((width,), F32),
                dma((10,)), dma((pieces,)), dma((nv,)), dma((nt,)), dma((pieces,)),
                dma, dma,
                dma((nt,)), dma((nt,)), dma((nt,)), dma((nt,)), dma((2,)), dma((2,)),
            ],
            compiler_params=pltpu.CompilerParams(
                collective_id=0, has_side_effects=True, vmem_limit_bytes=62 * 1024 * 1024
            ),
        )(frames, ln_gain, w_query, w_key, w_value, w_out, conv_gain, conv_weight)
    placed = (P("view", "tm", None, None), P(), P(), P(), P(), P(), P(), P("tm", None))
    return jax.shard_map(
        per_device, mesh=mesh, in_specs=placed, out_specs=P("view", "tm", None, None), check_vma=False
    )
```
